512 devices in a mesh: dp: 16 (over x, y), expert: 32 (over z, core).
Axes of the slice: x: 4, y: 4, z: 16, core: 2. Of those that a mesh axis runs over, the one named last changes fastest.
Arguments:
- tokens: bfloat16 [512, 196, 1280], P(('dp', 'expert')), may hold values from -40 to 40
- router: bfloat16 [1280, 32], replicated, may hold values from -2 to 2
- w_in: bfloat16 [32, 1280, 5120], P('expert', None, 'dp'), may hold values from -0.15625 to 0.15625
- w_out: bfloat16 [32, 5120, 1280], P('expert', 'dp'), may hold values from -0.078125 to 0.078125
- cotangent: bfloat16 [512, 196, 1280], P(('dp', 'expert')), may hold values from -6 to 6
Outputs:
- grad_tokens: bfloat16 [512, 196, 1280], P(('dp', 'expert'))
- grad_router: float32 [1280, 32], replicated
- grad_w_in: bfloat16 [32, 1280, 5120], P('expert', None, 'dp')
- grad_w_out: bfloat16 [32, 5120, 1280], P('expert', 'dp')
The draws below stay inside these ranges and needn't reach their ends.
All inputs are finite; a program needn't handle non-finite values.
Results may differ from the reference program's by a relative error of at most 0.022.
Values may be sent and summed in bfloat16 or wider, within the bound.
No kernel may reach another device: no remote copies, remote signals or barrier semaphores. Data moves between devices by JAX's collectives and lax.ppermute only.
A program may use at most 64 MiB of HBM per device.

```python
import math
import jax
import jax.numpy as jnp
from jax import lax

D = 1280
FF = 5120
TOKENS_IMG = 196
SLOTS = 32
IMAGES = 512
HID_DEV = 320
N_DP = 16


def shared_base(key):
    return jnp.clip(jax.random.normal(key, (D, SLOTS), jnp.float32), -4.0, 4.0)


def draw_router(key, part):
    base = shared_base(key)
    factor = 1.0
    return jnp.clip(base * (factor / math.sqrt(D)), -2.0, 2.0).astype(jnp.bfloat16)


def draw_tokens(key, part):
    key = jax.random.fold_in(key, 7)
    noise = jnp.clip(jax.random.normal(key, (IMAGES, TOKENS_IMG, D), jnp.float32), -6.0, 6.0)
    return jnp.clip(noise, -40.0, 40.0).astype(jnp.bfloat16)


def level_of(key, extent, split, least, top_value):
    def one(dim, blocks):
        steps = jax.random.uniform(jax.random.fold_in(jax.random.fold_in(key, 6), dim), (blocks,), jnp.float32, least / len(split), top_value / len(split))
        return jnp.repeat(jnp.exp(steps), extent[dim] // blocks).reshape((-1,) + (1,) * (len(extent) - dim - 1))

    level = one(*split[0])
    for cut in split[1:]:
        level = level * one(*cut)
    return level


def bell_draw(stream_key, extent, spread, limit, shards=(), kind=jnp.bfloat16):
    drawn = jax.random.normal(stream_key, extent, jnp.float32) * spread
    if len(shards) > 0:
        drawn = level_of(stream_key, extent, shards, -0.22, 0.18) * drawn
    return jnp.clip(drawn, min=-limit, max=limit).astype(kind)


def setup_inputs(seed: int = 0) -> dict:
    streams_of = jax.random.split(jax.random.key(seed), 6)
    tokens = draw_tokens(jax.random.fold_in(streams_of[5], 71), 0)
    router = draw_router(jax.random.fold_in(streams_of[5], 71), 0)
    w_in = bell_draw(streams_of[2], (SLOTS, D, FF), D ** -0.5, 0.15625, ((0, 32), (2, 16)))
    w_out = bell_draw(streams_of[3], (SLOTS, FF, D), FF ** -0.5, 0.078125, ((0, 32), (1, 16)))
    cotangent = bell_draw(streams_of[4], (IMAGES, TOKENS_IMG, D), 1.0, 6.0, ((0, 512),))
    return dict(tokens=tokens, router=router, w_in=w_in, w_out=w_out, cotangent=cotangent)


def gelu_slope(x):
    cdf = 0.5 * (1.0 + jax.scipy.special.erf(x * 0.7071067811865476))
    return cdf + x * jnp.exp(-0.5 * x * x) * 0.3989422804014327


def reference(tokens, router, w_in, w_out, cotangent):
    def router_fwd(image):
        logits = jnp.dot(image, router, preferred_element_type=jnp.float32)
        dispatch = jax.nn.softmax(logits, axis=0)
        combine = jax.nn.softmax(logits, axis=1)
        slot_in = jnp.dot(dispatch.astype(jnp.bfloat16).T, image, preferred_element_type=jnp.float32).astype(jnp.bfloat16)
        return dispatch, combine, slot_in

    dispatch, combine, slot_in = lax.map(router_fwd, tokens)

    def expert_fwd(inputs):
        inbound, weight_in, weight_out = inputs
        pre = jnp.dot(inbound, weight_in, preferred_element_type=jnp.float32)
        hidden = jax.nn.gelu(pre, approximate=False).astype(jnp.bfloat16)
        hblocks = hidden.astype(jnp.float32).reshape(IMAGES, N_DP, HID_DEV)
        wblocks = weight_out.astype(jnp.float32).reshape(N_DP, HID_DEV, D)
        parts = jnp.einsum('bnh,nhd->bnd', hblocks, wblocks).astype(jnp.bfloat16).astype(jnp.float32)
        return pre, hidden, jnp.sum(parts, axis=1).astype(jnp.bfloat16)

    slot_major = jnp.swapaxes(slot_in, 0, 1)
    pre, hidden, slot_out = lax.map(expert_fwd, (slot_major, w_in, w_out))
    slot_out_img = jnp.swapaxes(slot_out, 0, 1)

    def combine_all(inputs):
        comb, outs, grad_out = inputs
        comb_bf = comb.astype(jnp.bfloat16)
        g_comb = jnp.dot(grad_out, outs.T, preferred_element_type=jnp.float32)
        g_clog = comb * (g_comb - jnp.sum(comb * g_comb, axis=1, keepdims=True))
        g_sout = jnp.dot(comb_bf.T, grad_out, preferred_element_type=jnp.float32).astype(jnp.bfloat16)
        return g_clog, g_sout

    g_clog, g_sout = lax.map(combine_all, (combine, slot_out_img, cotangent))

    def expert_bwd(inputs):
        inbound, pre_s, hidden_s, grad_s, weight_in, weight_out = inputs
        g_hid = jnp.dot(grad_s, weight_out.T, preferred_element_type=jnp.float32)
        g_pre = (g_hid * gelu_slope(pre_s)).astype(jnp.bfloat16)
        grad_out_w = jnp.dot(hidden_s.T, grad_s, preferred_element_type=jnp.float32).astype(jnp.bfloat16)
        grad_in_w = jnp.dot(inbound.T, g_pre, preferred_element_type=jnp.float32).astype(jnp.bfloat16)
        gblocks = g_pre.astype(jnp.float32).reshape(IMAGES, N_DP, HID_DEV)
        wblocks = weight_in.astype(jnp.float32).reshape(D, N_DP, HID_DEV)
        parts = jnp.einsum('bnh,dnh->bnd', gblocks, wblocks).astype(jnp.bfloat16).astype(jnp.float32)
        return grad_in_w, grad_out_w, jnp.sum(parts, axis=1).astype(jnp.bfloat16)

    grad_w_in, grad_w_out, g_slot = lax.map(
        expert_bwd, (slot_major, pre, hidden, jnp.swapaxes(g_sout, 0, 1), w_in, w_out))
    g_slot_img = jnp.swapaxes(g_slot, 0, 1)

    def router_bwd(inputs):
        image, disp, clog, gslot = inputs
        g_disp = jnp.dot(image, gslot.T, preferred_element_type=jnp.float32)
        g_dlog = disp * (g_disp - jnp.sum(disp * g_disp, axis=0, keepdims=True))
        g_logits = (g_dlog + clog).astype(jnp.bfloat16)
        grad_image = jnp.dot(disp.astype(jnp.bfloat16), gslot, preferred_element_type=jnp.float32)
        grad_image = grad_image + jnp.dot(g_logits, router.T, preferred_element_type=jnp.float32)
        term = jnp.dot(image.T, g_logits, preferred_element_type=jnp.float32)
        return grad_image.astype(jnp.bfloat16), term

    grad_tokens, terms = lax.map(router_bwd, (tokens, dispatch, g_clog, g_slot_img))
    grad_router = jnp.sum(terms, axis=0)
    return grad_tokens, grad_router, grad_w_in, grad_w_out
```

```python
import jax
import jax.numpy as jnp
from jax import lax
from jax.sharding import PartitionSpec as P

BF = jnp.bfloat16
F32 = jnp.float32


def gelu_slope(x):
    cdf = 0.5 * (1.0 + jax.scipy.special.erf(x * 0.7071067811865476))
    return cdf + x * jnp.exp(-0.5 * x * x) * 0.3989422804014327


def dot(spec, a, b):
    return jnp.einsum(spec, a, b, preferred_element_type=F32)


def swap(x, axis):
    return lax.all_to_all(x, axis, split_axis=0, concat_axis=0, tiled=True)


def local(tokens, router, w_in, w_out, cotangent):
    n_dp, n_ex = lax.axis_size("dp"), lax.axis_size("expert")
    tok, cot = tokens[0], cotangent[0]
    win, wout = w_in[0], w_out[0]
    d = tok.shape[1]

    logits = dot("td,ds->ts", tok, router)
    dispatch = jax.nn.softmax(logits, axis=0)
    combine = jax.nn.softmax(logits, axis=1)
    dispatch_bf = dispatch.astype(BF)
    combine_bf = combine.astype(BF)
    slot_in = dot("ts,td->sd", dispatch_bf, tok).astype(BF)
    g_late = dot("ts,td->sd", combine_bf, cot).astype(BF)

    rows = swap(jnp.concatenate([slot_in, g_late], axis=1), "expert")
    rows = rows.reshape(n_ex, 2, d).transpose(1, 0, 2).reshape(2 * n_ex, d)
    every = swap(jnp.broadcast_to(rows[None], (n_dp, 2 * n_ex, d)), "dp")
    every = every.reshape(n_dp, 2, n_ex, d)
    all_in = every[:, 0].reshape(n_dp * n_ex, d)
    g_sall = every[:, 1].reshape(n_dp * n_ex, d)

    pre = dot("bd,dh->bh", all_in, win)
    hidden = jax.nn.gelu(pre, approximate=False).astype(BF)
    g_hid = dot("bd,hd->bh", g_sall, wout)
    g_pre = (g_hid * gelu_slope(pre)).astype(BF)
    slot_part = dot("bh,hd->bd", hidden, wout).astype(BF)
    g_slot_part = dot("bh,dh->bd", g_pre, win).astype(BF)
    grad_w_out = dot("bh,bd->hd", hidden, g_sall).astype(BF)
    grad_w_in = dot("bd,bh->dh", all_in, g_pre).astype(BF)

    terms = jnp.concatenate(
        [slot_part.reshape(n_dp, n_ex, d), g_slot_part.reshape(n_dp, n_ex, d)], axis=1
    )
    terms = swap(terms, "dp")
    sums = jnp.sum(terms.astype(F32), axis=0).astype(BF)
    sums = sums.reshape(2, n_ex, d).transpose(1, 0, 2).reshape(n_ex, 2 * d)
    back = swap(sums, "expert")
    slot_out, g_slot = back[:, :d], back[:, d:]

    g_comb = dot("td,sd->ts", cot, slot_out)
    g_clog = combine * (g_comb - jnp.sum(combine * g_comb, axis=1, keepdims=True))
    g_disp = dot("td,sd->ts", tok, g_slot)
    g_dlog = dispatch * (g_disp - jnp.sum(dispatch * g_disp, axis=0, keepdims=True))
    g_logits = (g_dlog + g_clog).astype(BF)

    term = dot("ts,td->sd", g_logits, tok)
    row = jnp.sum(swap(term, "expert"), axis=0, keepdims=True)
    row = jnp.sum(swap(jnp.broadcast_to(row, (n_dp, d)), "dp"), axis=0, keepdims=True)
    grad_router = swap(jnp.broadcast_to(row, (n_ex, d)), "expert").T

    grad_tokens = dot("ts,sd->td", dispatch_bf, g_slot) + dot("ts,ds->td", g_logits, router)
    return (grad_tokens.astype(BF)[None], grad_router, grad_w_in[None], grad_w_out[None])


def solution(mesh):
    placed = (
        P(("dp", "expert"), None, None),
        P(),
        P("expert", None, "dp"),
        P("expert", "dp", None),
        P(("dp", "expert"), None, None),
    )
    return jax.shard_map(
        local,
        mesh=mesh,
        in_specs=placed,
        out_specs=(
            P(("dp", "expert"), None, None),
            P(),
            P("expert", None, "dp"),
            P("expert", "dp", None),
        ),
        check_vma=False,
    )
```

```python
import jax
import jax.numpy as jnp
import numpy as np
from jax import lax
from jax.sharding import Mesh, PartitionSpec as P

BF = jnp.bfloat16
F32 = jnp.float32
PLANE = ("x", "yh", "yl")
CHIPS = ("x", "yh", "yl", "core")
TURN = [(0, 0), (1, 2), (2, 1), (3, 3)]
OTHER = [(0, 1), (1, 0)]


def gelu_slope(x):
    cdf = 0.5 * (1.0 + jax.scipy.special.erf(x * 0.7071067811865476))
    return cdf + x * jnp.exp(-0.5 * x * x) * 0.3989422804014327


def dot(spec, a, b):
    return jnp.einsum(spec, a, b, preferred_element_type=F32)


def swap(x, axis):
    return lax.all_to_all(x, axis, split_axis=0, concat_axis=0, tiled=True)


def local(tokens, router, w_in, w_out, cotangent):
    n_z = lax.axis_size("z")
    n_plane = lax.axis_size(PLANE)
    n_chips = lax.axis_size(CHIPS)
    tok, cot = tokens[0], cotangent[0]
    d = tok.shape[1]
    hid = w_out.shape[1]

    held = jnp.concatenate([w_in[0].T, w_out[0]], axis=0)
    mine = lax.ppermute(held, ("yl", "core"), TURN)
    other = lax.ppermute(mine, "core", OTHER)

    logits = dot("td,ds->ts", tok, router)
    dispatch = jax.nn.softmax(logits, axis=0)
    combine = jax.nn.softmax(logits, axis=1)
    dispatch_bf = dispatch.astype(BF)
    combine_bf = combine.astype(BF)
    slot_in = dot("ts,td->sd", dispatch_bf, tok).astype(BF)
    g_late = dot("ts,td->sd", combine_bf, cot).astype(BF)

    rows = jnp.stack([slot_in.reshape(n_z, 2, d), g_late.reshape(n_z, 2, d)], axis=2)
    rows = swap(rows.reshape(n_z, 4, d), "z").reshape(n_z, 2, 2, d)
    rows = rows.transpose(1, 2, 0, 3).reshape(1, 2, 2 * n_z, d)
    every = jnp.broadcast_to(rows, (n_plane // 2, 2, 2 * n_z, d)).reshape(n_plane, 2 * n_z, d)
    every = swap(every, PLANE).reshape(n_plane, 2, n_z, d)
    all_in = every[:, 0].reshape(n_plane * n_z, d)
    g_sall = every[:, 1].reshape(n_plane * n_z, d)

    slot_part, g_slot_part, kept = 0.0, 0.0, []
    for block in (mine, other):
        win, wout = block[:hid], block[hid:]
        pre = dot("bd,hd->bh", all_in, win)
        hidden = jax.nn.gelu(pre, approximate=False).astype(BF)
        g_pre = (dot("bd,hd->bh", g_sall, wout) * gelu_slope(pre)).astype(BF)
        slot_part = slot_part + dot("bh,hd->bd", hidden, wout)
        g_slot_part = g_slot_part + dot("bh,hd->bd", g_pre, win)
        kept.append((hidden, g_pre))

    terms = jnp.concatenate(
        [
            slot_part.astype(BF).reshape(n_plane, n_z, d),
            g_slot_part.astype(BF).reshape(n_plane, n_z, d),
        ],
        axis=1,
    )
    terms = swap(terms, PLANE).reshape(n_plane // 2, 2, 2, n_z, d)
    sums = jnp.sum(terms.astype(F32), axis=0).astype(BF)
    sums = sums.transpose(2, 0, 1, 3).reshape(n_z, 4, d)
    back = swap(sums, "z").reshape(n_z, 2, 2, d)
    slot_out, g_slot = back[:, :, 0].reshape(2 * n_z, d), back[:, :, 1].reshape(2 * n_z, d)

    grads = []
    for hidden, g_pre in kept:
        grads.append(
            jnp.concatenate([dot("bh,bd->hd", g_pre, all_in), dot("bh,bd->hd", hidden, g_sall)], axis=0)
        )
    theirs = lax.ppermute(grads[1].astype(BF), "core", OTHER)
    whole = (grads[0] + theirs.astype(F32)).astype(BF)
    whole = lax.ppermute(whole, ("yl", "core"), TURN)
    grad_w_in, grad_w_out = whole[:hid].T, whole[hid:]

    g_comb = dot("td,sd->ts", cot, slot_out)
    g_clog = combine * (g_comb - jnp.sum(combine * g_comb, axis=1, keepdims=True))
    g_disp = dot("td,sd->ts", tok, g_slot)
    g_dlog = dispatch * (g_disp - jnp.sum(dispatch * g_disp, axis=0, keepdims=True))
    g_logits = (g_dlog + g_clog).astype(BF)

    term = dot("ts,td->sd", g_logits, tok)
    row = jnp.sum(swap(term, CHIPS), axis=0, keepdims=True)
    row = jnp.sum(swap(jnp.broadcast_to(row, (n_z, d)), "z"), axis=0, keepdims=True)
    grad_router = swap(jnp.broadcast_to(row, (n_chips, d)), CHIPS).T

    grad_tokens = dot("ts,sd->td", dispatch_bf, g_slot) + dot("ts,ds->td", g_logits, router)
    return (grad_tokens.astype(BF)[None], grad_router, grad_w_in[None], grad_w_out[None])


def solution(mesh):
    fine = Mesh(np.asarray(mesh.devices).reshape(4, 2, 2, 16, 2), ("x", "yh", "yl", "z", "core"))
    images = P(("x", "yh", "yl", "z", "core"), None, None)
    first = P(("z", "core"), None, ("x", "yh", "yl"))
    second = P(("z", "core"), ("x", "yh", "yl"), None)
    return jax.shard_map(
        local,
        mesh=fine,
        in_specs=(images, P(), first, second, images),
        out_specs=(images, P(), first, second),
        check_vma=False,
    )
```

```python
import jax
import jax.numpy as jnp
import numpy as np
from jax import lax
from jax.experimental import pallas as pl
from jax.experimental.pallas import tpu as pltpu
from jax.sharding import Mesh, PartitionSpec as P

BF = jnp.bfloat16
F32 = jnp.float32
PLANE = ("x", "yh", "yl")
CHIPS = ("x", "yh", "yl", "core")
TURN = [(2, 0), (0, 1), (1, 3), (3, 2)]
BACK = [(b, a) for a, b in TURN]
OTHER = [(0, 1), (1, 0)]


def dot(spec, a, b):
    return jnp.einsum(spec, a, b, preferred_element_type=F32)


def nn(a, b):
    return jnp.dot(a, b, preferred_element_type=F32)


def nt(a, b):
    return lax.dot_general(a, b, (((1,), (1,)), ((), ())), preferred_element_type=F32)


def tn(a, b):
    return lax.dot_general(a, b, (((0,), (0,)), ((), ())), preferred_element_type=F32)


def rows_of(every):
    n, both, d = every.shape
    half = both // 2
    return every[:, :half].reshape(n * half, d), every[:, half:].reshape(n * half, d)


def expert_kernel(every, mine, other, terms, hidden, g_pre):
    hid = mine.shape[0] // 2
    n, both, d = every.shape
    x, g = rows_of(every[...])
    out, back = 0.0, 0.0
    for i, block in enumerate((mine, other)):
        win, wout = block[:hid], block[hid:]
        pre = nt(x, win)
        cdf = 0.5 * (1.0 + lax.erf(pre * 0.7071067811865476))
        h = (pre * cdf).astype(BF)
        slope = cdf + pre * jnp.exp(-0.5 * pre * pre) * 0.3989422804014327
        gp = (nt(g, wout) * slope).astype(BF)
        hidden[i] = h
        g_pre[i] = gp
        out = out + nn(h, wout)
        back = back + nn(gp, win)
    terms[:, : both // 2] = out.astype(BF).reshape(n, both // 2, d)
    terms[:, both // 2 :] = back.astype(BF).reshape(n, both // 2, d)


def other_kernel(every, hidden, g_pre, grads):
    hid = grads.shape[0] // 2
    x, g = rows_of(every[...])
    grads[:hid] = tn(g_pre[1], x).astype(BF)
    grads[hid:] = tn(hidden[1], g).astype(BF)


def mine_kernel(every, hidden, g_pre, theirs, grads):
    hid = grads.shape[0] // 2
    x, g = rows_of(every[...])
    grads[:hid] = (tn(g_pre[0], x) + theirs[:hid].astype(F32)).astype(BF)
    grads[hid:] = (tn(hidden[0], g) + theirs[hid:].astype(F32)).astype(BF)


def call(kernel, outs, flops, *args):
    moved = sum(a.size * a.dtype.itemsize for a in args) + sum(o.size * o.dtype.itemsize for o in outs)
    whole = pl.BlockSpec(memory_space=pltpu.VMEM)
    return pl.pallas_call(
        kernel,
        out_shape=outs,
        in_specs=[whole] * len(args),
        out_specs=[whole] * len(outs),
        compiler_params=pltpu.CompilerParams(vmem_limit_bytes=28 * 2**20),
        cost_estimate=pl.CostEstimate(flops=flops, bytes_accessed=moved, transcendentals=0),
    )(*args)


def swap(x, axis):
    return lax.all_to_all(x, axis, split_axis=0, concat_axis=0, tiled=True)


def local(tokens, router, w_in, w_out, cotangent):
    n_z = lax.axis_size("z")
    n_plane = lax.axis_size(PLANE)
    n_chips = lax.axis_size(CHIPS)
    tok, cot = tokens[0], cotangent[0]
    d = tok.shape[1]
    hid = w_out.shape[1]

    held = jnp.concatenate([w_in[0].T, w_out[0]], axis=0)
    mine = lax.ppermute(held, ("yl", "core"), TURN)
    other = lax.ppermute(mine, "core", OTHER)

    logits = dot("td,ds->ts", tok, router)
    dispatch = jax.nn.softmax(logits, axis=0)
    combine = jax.nn.softmax(logits, axis=1)
    dispatch_bf = dispatch.astype(BF)
    combine_bf = combine.astype(BF)
    slot_in = dot("ts,td->sd", dispatch_bf, tok).astype(BF)
    g_late = dot("ts,td->sd", combine_bf, cot).astype(BF)

    rows = jnp.stack([slot_in.reshape(n_z, 2, d), g_late.reshape(n_z, 2, d)], axis=2)
    rows = swap(rows.reshape(n_z, 4, d), "z").reshape(n_z, 2, 2, d)
    rows = rows.transpose(1, 2, 0, 3).reshape(1, 2, 2 * n_z, d)
    every = jnp.broadcast_to(rows, (n_plane // 2, 2, 2 * n_z, d)).reshape(n_plane, 2 * n_z, d)
    every = swap(every, PLANE)
    n_rows = n_plane * n_z
    unit = jax.ShapeDtypeStruct((2, n_rows, hid), BF)
    block = jax.ShapeDtypeStruct(mine.shape, BF)
    work = 2 * n_rows * hid * d
    terms, hidden, g_pre = call(
        expert_kernel,
        [jax.ShapeDtypeStruct(every.shape, BF), unit, unit],
        8 * work,
        every,
        mine,
        other,
    )

    terms = swap(terms, PLANE).reshape(n_plane // 2, 2, 2, n_z, d)
    sums = jnp.sum(terms.astype(F32), axis=0).astype(BF)
    sums = sums.transpose(2, 0, 1, 3).reshape(n_z, 4, d)
    back = swap(sums, "z").reshape(n_z, 2, 2, d)
    slot_out, g_slot = back[:, :, 0].reshape(2 * n_z, d), back[:, :, 1].reshape(2 * n_z, d)

    (theirs,) = call(other_kernel, [block], 2 * work, every, hidden, g_pre)
    theirs = lax.ppermute(theirs, "core", OTHER)
    (home,) = call(mine_kernel, [block], 2 * work, every, hidden, g_pre, theirs)
    home = lax.ppermute(home, ("yl", "core"), BACK)

    g_comb = dot("td,sd->ts", cot, slot_out)
    g_clog = combine * (g_comb - jnp.sum(combine * g_comb, axis=1, keepdims=True))
    g_disp = dot("td,sd->ts", tok, g_slot)
    g_dlog = dispatch * (g_disp - jnp.sum(dispatch * g_disp, axis=0, keepdims=True))
    g_logits = (g_dlog + g_clog).astype(BF)

    term = dot("ts,td->sd", g_logits, tok)
    row = jnp.sum(swap(term, CHIPS), axis=0, keepdims=True)
    row = jnp.sum(swap(jnp.broadcast_to(row, (n_z, d)), "z"), axis=0, keepdims=True)
    row, home = lax.optimization_barrier((row, home))
    grad_w_in, grad_w_out = home[:hid].T, home[hid:]
    grad_router = swap(jnp.broadcast_to(row, (n_chips, d)), CHIPS).T

    grad_tokens = dot("ts,sd->td", dispatch_bf, g_slot) + dot("ts,ds->td", g_logits, router)
    return (grad_tokens.astype(BF)[None], grad_router, grad_w_in[None], grad_w_out[None])


def solution(mesh):
    fine = Mesh(np.asarray(mesh.devices).reshape(4, 2, 2, 16, 2), ("x", "yh", "yl", "z", "core"))
    images = P(("x", "yh", "yl", "z", "core"), None, None)
    first = P(("z", "core"), None, ("x", "yh", "yl"))
    second = P(("z", "core"), ("x", "yh", "yl"), None)
    return jax.shard_map(
        local,
        mesh=fine,
        in_specs=(images, P(), first, second, images),
        out_specs=(images, P(), first, second),
        check_vma=False,
    )
```

```python
import jax
import jax.numpy as jnp
import numpy as np
from jax import lax
from jax.experimental import pallas as pl
from jax.experimental.pallas import tpu as pltpu
from jax.sharding import Mesh, PartitionSpec as P

BF = jnp.bfloat16
F32 = jnp.float32
PLANE = ("x", "yh", "yl")
CHIPS = ("x", "yh", "yl", "core")
PAIR = ("yl", "core")
TURN = [(2, 0), (0, 1), (1, 3), (3, 2)]
BACK = [(b, a) for a, b in TURN]
OTHER = [(0, 1), (1, 0)]


def dot(spec, a, b):
    return jnp.einsum(spec, a, b, preferred_element_type=F32)


def nn(a, b):
    return jnp.dot(a, b, preferred_element_type=F32)


def nt(a, b):
    return lax.dot_general(a, b, (((1,), (1,)), ((), ())), preferred_element_type=F32)


def tn(a, b):
    return lax.dot_general(a, b, (((0,), (0,)), ((), ())), preferred_element_type=F32)


def rows_of(every):
    n, both, d = every.shape
    half = both // 2
    return every[:, :half].reshape(n * half, d), every[:, half:].reshape(n * half, d)


def expert_kernel(every, mine, in1, out1, terms, rows, hidden, g_pre, h_part, g_part, sems):
    hid = mine.shape[0] // 2
    n, both, d = every.shape
    saves = [pltpu.make_async_copy(every, rows, sems.at[0])]
    saves[0].start()
    x, g = rows_of(every[...])
    out, back = 0.0, 0.0
    for i, (win, wout) in enumerate(((mine[:hid], mine[hid:]), (in1[...], out1[...]))):
        pre = nt(x, win)
        cdf = 0.5 * (1.0 + lax.erf(pre * 0.7071067811865476))
        h = (pre * cdf).astype(BF)
        slope = cdf + pre * jnp.exp(-0.5 * pre * pre) * 0.3989422804014327
        gp = (nt(g, wout) * slope).astype(BF)
        h_part[i] = h
        g_part[i] = gp
        saves.append(pltpu.make_async_copy(h_part.at[i], hidden.at[i], sems.at[1 + 2 * i]))
        saves.append(pltpu.make_async_copy(g_part.at[i], g_pre.at[i], sems.at[2 + 2 * i]))
        saves[-2].start()
        saves[-1].start()
        out = out + nn(h, wout)
        back = back + nn(gp, win)
    terms[:, : both // 2] = out.astype(BF).reshape(n, both // 2, d)
    terms[:, both // 2 :] = back.astype(BF).reshape(n, both // 2, d)
    for save in saves:
        save.wait()


def grads_kernel(every, hidden, g_pre, kept, given):
    hid = kept.shape[0] // 2
    x, g = rows_of(every[...])
    for i, grads in enumerate((kept, given)):
        grads[:hid] = tn(g_pre[i], x).astype(BF)
        grads[hid:] = tn(hidden[i], g).astype(BF)


def add_kernel(kept, given, grads_in, grads_out):
    hid = grads_in.shape[0]
    grads_in[...] = (kept[:hid].astype(F32) + given[:hid].astype(F32)).astype(BF)
    grads_out[...] = (kept[hid:].astype(F32) + given[hid:].astype(F32)).astype(BF)


def place_kernel(a, b, a_out, b_out):
    a_out[...] = a[...]
    b_out[...] = b[...]


def sum_kernel(terms, sums):
    n, both, d = terms.shape
    n_z = both // 2
    for parity in range(2):
        for kind in range(2):
            total = 0.0
            for chip in range(parity, n, 2):
                total = total + terms[chip, kind * n_z : (kind + 1) * n_z].astype(F32)
            sums[:, parity * 2 + kind] = total.astype(BF)


def call(kernel, outs, flops, *args, saved=(), scratch=(), vmem=8):
    moved = sum(a.size * a.dtype.itemsize for a in (*args, *outs, *saved))
    whole = pl.BlockSpec(memory_space=pltpu.VMEM)
    return pl.pallas_call(
        kernel,
        out_shape=[*outs, *(pltpu.HBM(a.shape, a.dtype) for a in saved)],
        in_specs=[whole] * len(args),
        out_specs=[whole] * len(outs) + [pl.BlockSpec(memory_space=pltpu.HBM)] * len(saved),
        scratch_shapes=scratch,
        compiler_params=pltpu.CompilerParams(vmem_limit_bytes=vmem * 2**20),
        cost_estimate=pl.CostEstimate(flops=flops, bytes_accessed=moved, transcendentals=0),
    )(*args)


def swap(x, axis):
    return lax.all_to_all(x, axis, split_axis=0, concat_axis=0, tiled=True)


def local(tokens, router, w_in, w_out, cotangent):
    n_z = lax.axis_size("z")
    n_plane = lax.axis_size(PLANE)
    n_chips = lax.axis_size(CHIPS)
    tok, cot = tokens[0], cotangent[0]
    d = tok.shape[1]
    hid = w_out.shape[1]

    logits = dot("td,ds->ts", tok, router)
    dispatch = jax.nn.softmax(logits, axis=0)
    combine = jax.nn.softmax(logits, axis=1)
    dispatch_bf = dispatch.astype(BF)
    combine_bf = combine.astype(BF)
    slot_in = dot("ts,td->sd", dispatch_bf, tok).astype(BF)
    g_late = dot("ts,td->sd", combine_bf, cot).astype(BF)

    rows = jnp.stack([slot_in.reshape(n_z, 2, d), g_late.reshape(n_z, 2, d)], axis=2)
    rows = rows.reshape(n_z, 4, d)
    rows, win, wout = lax.optimization_barrier((rows, w_in[0].T, w_out[0]))
    mine = lax.ppermute(jnp.concatenate([win, wout], axis=0), PAIR, TURN)
    rows = swap(rows, "z")
    in1 = lax.ppermute(mine[:hid], "core", OTHER)
    out1 = lax.ppermute(mine[hid:], "core", OTHER)
    rows = rows.reshape(n_z, 2, 2, d)
    rows = rows.transpose(1, 2, 0, 3).reshape(1, 2, 2 * n_z, d)
    every = jnp.broadcast_to(rows, (n_plane // 2, 2, 2 * n_z, d)).reshape(n_plane, 2 * n_z, d)
    every = swap(every, PLANE)
    n_rows = n_plane * n_z
    unit = jax.ShapeDtypeStruct((2, n_rows, hid), BF)
    block = jax.ShapeDtypeStruct((2 * hid, d), BF)
    half = jax.ShapeDtypeStruct((hid, d), BF)
    work = 2 * n_rows * hid * d
    terms, rows, hidden, g_pre = call(
        expert_kernel,
        [jax.ShapeDtypeStruct(every.shape, BF)],
        8 * work,
        every,
        mine,
        in1,
        out1,
        saved=[every, unit, unit],
        scratch=[pltpu.VMEM(unit.shape, BF)] * 2 + [pltpu.SemaphoreType.DMA((5,))],
        vmem=16,
    )
    kept, given = call(grads_kernel, [block, block], 4 * work, rows, hidden, g_pre, vmem=12)
    given = lax.ppermute(given, "core", OTHER)

    terms = swap(terms, PLANE)
    (sums,) = call(sum_kernel, [jax.ShapeDtypeStruct((n_z, 4, d), BF)], terms.size, terms)
    home_in, home_out = call(add_kernel, [half, half], block.size, kept, given)
    home_in = lax.ppermute(home_in, PAIR, BACK)
    back = swap(sums, "z").reshape(n_z, 2, 2, d)
    slot_out, g_slot = back[:, :, 0].reshape(2 * n_z, d), back[:, :, 1].reshape(2 * n_z, d)

    g_comb = dot("td,sd->ts", cot, slot_out)
    g_clog = combine * (g_comb - jnp.sum(combine * g_comb, axis=1, keepdims=True))
    g_disp = dot("td,sd->ts", tok, g_slot)
    g_dlog = dispatch * (g_disp - jnp.sum(dispatch * g_disp, axis=0, keepdims=True))
    g_logits = (g_dlog + g_clog).astype(BF)

    term = dot("ts,td->sd", g_logits, tok)
    row, home_in, home_out = lax.optimization_barrier((swap(term, CHIPS), home_in, home_out))
    home_out = lax.ppermute(home_out, PAIR, BACK)
    row = jnp.sum(row, axis=0, keepdims=True)
    row = jnp.sum(swap(jnp.broadcast_to(row, (n_z, d)), "z"), axis=0, keepdims=True)
    row, home_in, home_out = lax.optimization_barrier((row, home_in, home_out))
    grad_w_in, grad_w_out = call(place_kernel, [half, half], block.size, home_in, home_out)
    grad_router = swap(jnp.broadcast_to(row, (n_chips, d)), CHIPS).T

    grad_tokens = dot("ts,sd->td", dispatch_bf, g_slot) + dot("ts,ds->td", g_logits, router)
    return (grad_tokens.astype(BF)[None], grad_router, grad_w_in.T[None], grad_w_out[None])


def solution(mesh):
    fine = Mesh(np.asarray(mesh.devices).reshape(4, 2, 2, 16, 2), ("x", "yh", "yl", "z", "core"))
    images = P(("x", "yh", "yl", "z", "core"), None, None)
    first = P(("z", "core"), None, ("x", "yh", "yl"))
    second = P(("z", "core"), ("x", "yh", "yl"), None)
    return jax.shard_map(
        local,
        mesh=fine,
        in_specs=(images, P(), first, second, images),
        out_specs=(images, P(), first, second),
        check_vma=False,
    )
```

```python
import jax
import jax.numpy as jnp
import numpy as np
from jax import lax
from jax.experimental import pallas as pl
from jax.experimental.pallas import tpu as pltpu
from jax.sharding import Mesh, PartitionSpec as P

BF = jnp.bfloat16
F32 = jnp.float32
PLANE = ("x", "yh", "yl")
CHIPS = ("x", "yh", "yl", "core")
PAIR = ("yl", "core")
TURN = [(2, 0), (0, 1), (1, 3), (3, 2)]
BACK = [(b, a) for a, b in TURN]
OTHER = [(0, 1), (1, 0)]


def nn(a, b):
    return jnp.dot(a, b, preferred_element_type=F32)


def nt(a, b):
    return lax.dot_general(a, b, (((1,), (1,)), ((), ())), preferred_element_type=F32)


def tn(a, b):
    return lax.dot_general(a, b, (((0,), (0,)), ((), ())), preferred_element_type=F32)


def dot(spec, a, b):
    return jnp.einsum(spec, a, b, preferred_element_type=F32)


def rows_of(every):
    n, both, d = every.shape
    half = both // 2
    return every[:, :half].reshape(n * half, d), every[:, half:].reshape(n * half, d)


def reorder(slots):
    n_z = slots // 2
    row = lax.broadcasted_iota(jnp.int32, (slots, slots), 0)
    column = lax.broadcasted_iota(jnp.int32, (slots, slots), 1)
    last = (row >= n_z).astype(jnp.int32)
    return (column == 2 * (row - n_z * last) + last).astype(F32).astype(BF)


def expert_kernel(every, mine, other, terms, rows, hidden, g_pre, h_part, g_part, win, wout, made, sems):
    hid = mine.shape[0] // 2
    n, both, d = every.shape
    half = both // 2
    loads = [pltpu.make_async_copy(other.at[:hid], win, sems.at[0]), pltpu.make_async_copy(other.at[hid:], wout, sems.at[1])]
    for load in loads:
        load.start()
    saves = [pltpu.make_async_copy(every, rows, sems.at[2])]
    saves[0].start()
    x, g = rows_of(every[...])
    for i in range(2):
        if i == 0:
            a, b = mine[:hid], mine[hid:]
        else:
            for load in loads:
                load.wait()
            a, b = win[...], wout[...]
        pre = nt(x, a)
        cdf = 0.5 * (1.0 + lax.erf(pre * 0.7071067811865476))
        h_part[i] = (pre * cdf).astype(BF)
        slope = cdf + pre * jnp.exp(-0.5 * pre * pre) * 0.3989422804014327
        g_part[i] = (nt(g, b) * slope).astype(BF)
        saves.append(pltpu.make_async_copy(h_part.at[i], hidden.at[i], sems.at[3 + 2 * i]))
        saves.append(pltpu.make_async_copy(g_part.at[i], g_pre.at[i], sems.at[4 + 2 * i]))
        saves[-2].start()
        saves[-1].start()
    out = nn(h_part[0], mine[hid:]) + nn(h_part[1], wout[...])
    made[:, :half] = out.astype(BF).reshape(n, half, d)
    saves.append(pltpu.make_async_copy(made.at[:, :half], terms.at[:, :half], sems.at[7]))
    saves[-1].start()
    back = nn(g_part[0], mine[:hid]) + nn(g_part[1], win[...])
    made[:, half:] = back.astype(BF).reshape(n, half, d)
    saves.append(pltpu.make_async_copy(made.at[:, half:], terms.at[:, half:], sems.at[8]))
    saves[-1].start()
    for save in saves:
        save.wait()


def grads_kernel(every, hidden, g_pre, kept, given):
    hid = kept.shape[0] // 2
    x, g = rows_of(every[...])
    for i, grads in enumerate((kept, given)):
        grads[:hid] = tn(g_pre[i], x).astype(BF)
        grads[hid:] = tn(hidden[i], g).astype(BF)


def add_kernel(kept, given, grads_in, grads_out):
    hid = grads_in.shape[0]
    grads_in[...] = (kept[:hid].astype(F32) + given[:hid].astype(F32)).astype(BF)
    grads_out[...] = (kept[hid:].astype(F32) + given[hid:].astype(F32)).astype(BF)


def place_kernel(a, b, a_out, b_out):
    a_out[...] = a[...]
    b_out[...] = b[...]


def sum_kernel(terms, sums, made, sem):
    n, both, d = terms.shape
    n_z = both // 2
    for core in range(2):
        for kind in range(2):
            total = 0.0
            for chip in range(core, n, 2):
                total = total + terms[chip, kind * n_z : (kind + 1) * n_z].astype(F32)
            made[:, core * 2 + kind] = total.astype(BF)
    send = pltpu.make_async_copy(made, sums, sem)
    send.start()
    send.wait()


def tail_kernel(back, tok, cot, dispatch, combine, term, g_logits, g_slot):
    turn = reorder(2 * back.shape[0])
    slot_out = tn(turn, jnp.concatenate([back[:, 0], back[:, 2]], axis=0)).astype(BF)
    slot_grad = tn(turn, jnp.concatenate([back[:, 1], back[:, 3]], axis=0)).astype(BF)
    com, dis = combine[...], dispatch[...]
    g_comb = nt(slot_out, cot[...])
    g_clog = com * (g_comb - jnp.sum(com * g_comb, axis=0, keepdims=True))
    g_disp = nt(slot_grad, tok[...])
    g_dlog = dis * (g_disp - jnp.sum(dis * g_disp, axis=1, keepdims=True))
    g_log = (g_dlog + g_clog).astype(BF)
    g_logits[...] = g_log
    g_slot[...] = slot_grad
    term[:, 0] = nn(g_log, tok[...])


def tokens_kernel(dispatch, g_logits, g_slot, router, grads):
    made = tn(dispatch[...].astype(BF), g_slot[...]) + tn(g_logits[...], router[...])
    grads[...] = made.astype(BF)


def total_near_kernel(parts, out):
    out[...] = jnp.broadcast_to(jnp.sum(parts[...], axis=0, keepdims=True), out.shape)


def total_kernel(parts, out, made, sem):
    total = jnp.sum(parts[...], axis=0, keepdims=True)
    made[...] = jnp.broadcast_to(total, made.shape)
    send = pltpu.make_async_copy(made, out, sem)
    send.start()
    send.wait()


def call(kernel, outs, flops, *args, saved=(), scratch=(), far=(), vmem=8):
    moved = sum(a.size * a.dtype.itemsize for a in (*args, *outs, *saved))
    whole = pl.BlockSpec(memory_space=pltpu.VMEM)
    return pl.pallas_call(
        kernel,
        out_shape=[*outs, *(pltpu.HBM(a.shape, a.dtype) for a in saved)],
        in_specs=[pl.BlockSpec(memory_space=pltpu.HBM) if i in far else whole for i in range(len(args))],
        out_specs=[whole] * len(outs) + [pl.BlockSpec(memory_space=pltpu.HBM)] * len(saved),
        scratch_shapes=scratch,
        compiler_params=pltpu.CompilerParams(vmem_limit_bytes=vmem * 2**20),
        cost_estimate=pl.CostEstimate(flops=flops, bytes_accessed=moved, transcendentals=0),
    )(*args)


def like(shape, kind=BF):
    return jax.ShapeDtypeStruct(shape, kind)


def swap(x, axis):
    return lax.all_to_all(x, axis, split_axis=0, concat_axis=0, tiled=True)


def local(tokens, router, w_in, w_out, cotangent):
    n_z = lax.axis_size("z")
    n_plane = lax.axis_size(PLANE)
    n_chips = lax.axis_size(CHIPS)
    tok, cot = tokens[0], cotangent[0]
    n_tok, d = tok.shape
    slots = 2 * n_z
    hid = w_out.shape[1]
    dma = pltpu.SemaphoreType.DMA
    one = 2 * n_tok * slots * d

    logits = dot("td,ds->ts", tok, router)
    dispatch = jax.nn.softmax(logits, axis=0)
    combine = jax.nn.softmax(logits, axis=1)
    slot_in = dot("ts,td->sd", dispatch.astype(BF), tok).astype(BF)
    g_late = dot("ts,td->sd", combine.astype(BF), cot).astype(BF)

    rows = jnp.stack([slot_in.reshape(n_z, 2, d), g_late.reshape(n_z, 2, d)], axis=2).reshape(n_z, 4, d)
    mine = lax.ppermute(jnp.concatenate([w_in[0].T, w_out[0]], axis=0), PAIR, TURN)
    rows = swap(rows, "z")
    other = lax.ppermute(mine, "core", OTHER)
    rows = rows.reshape(n_z, 2, 2, d).transpose(1, 2, 0, 3).reshape(1, 2, 2 * n_z, d)
    both = like((n_plane, 2 * n_z, d))
    every = jnp.broadcast_to(rows, (n_plane // 2, 2, 2 * n_z, d)).reshape(both.shape)
    every = swap(every, PLANE)
    n_rows = n_plane * n_z
    unit = like((2, n_rows, hid))
    block = like((2 * hid, d))
    half = like((hid, d))
    work = 2 * n_rows * hid * d
    terms, rows, hidden, g_pre = call(
        expert_kernel,
        [],
        8 * work,
        every,
        mine,
        other,
        far=(2,),
        saved=[both, both, unit, unit],
        scratch=[pltpu.VMEM(a.shape, BF) for a in (unit, unit, half, half, both)] + [dma((9,))],
        vmem=16,
    )
    kept, given = call(grads_kernel, [block, block], 4 * work, rows, hidden, g_pre, vmem=12)
    given = lax.ppermute(given, "core", OTHER)

    terms = swap(terms, PLANE)
    (sums,) = call(
        sum_kernel,
        [],
        400 * one,
        terms,
        saved=[like((n_z, 4, d))],
        scratch=[pltpu.VMEM((n_z, 4, d), BF), dma],
    )
    home_in, home_out = call(add_kernel, [half, half], block.size, kept, given)
    home_in = lax.ppermute(home_in, PAIR, BACK)
    back = swap(sums, "z")
    term, g_logits, g_slot = call(
        tail_kernel,
        [like((slots, 1, d), F32), like((slots, n_tok)), like((slots, d))],
        400 * one,
        back,
        tok,
        cot,
        dispatch.T,
        combine.T,
    )

    term = swap(term, CHIPS)
    row, home_in, home_out = lax.optimization_barrier((term, home_in, home_out))
    home_out = lax.ppermute(home_out, PAIR, BACK)
    (row,) = call(total_near_kernel, [like((n_z, 1, d), F32)], row.size, row)
    (row,) = call(
        total_kernel,
        [],
        400 * one,
        swap(row, "z"),
        saved=[like((n_chips, 1, d), F32)],
        scratch=[pltpu.VMEM((n_chips, 1, d), F32), dma],
    )
    row, home_in, home_out = lax.optimization_barrier((row, home_in, home_out))
    grad_w_in, grad_w_out = call(place_kernel, [half, half], block.size, home_in, home_out)
    grad_router = swap(row, CHIPS).reshape(n_chips, d).T
    (grad_tokens,) = call(tokens_kernel, [like((n_tok, d))], 2 * one, dispatch.T, g_logits, g_slot, router.T)
    return (grad_tokens[None], grad_router, grad_w_in.T[None], grad_w_out[None])


def solution(mesh):
    fine = Mesh(np.asarray(mesh.devices).reshape(4, 2, 2, 16, 2), ("x", "yh", "yl", "z", "core"))
    images = P(("x", "yh", "yl", "z", "core"), None, None)
    first = P(("z", "core"), None, ("x", "yh", "yl"))
    second = P(("z", "core"), ("x", "yh", "yl"), None)
    return jax.shard_map(
        local,
        mesh=fine,
        in_specs=(images, P(), first, second, images),
        out_specs=(images, P(), first, second),
        check_vma=False,
    )
```

```python
import jax
import jax.numpy as jnp
import numpy as np
from jax import lax
from jax.experimental import pallas as pl
from jax.experimental.pallas import tpu as pltpu
from jax.sharding import Mesh, PartitionSpec as P

BF = jnp.bfloat16
F32 = jnp.float32
PLANE = ("x", "yh", "yl")
CHIPS = ("x", "yh", "yl", "core")
PAIR = ("yl", "core")
TURN = [(2, 0), (0, 1), (1, 3), (3, 2)]
BACK = [(b, a) for a, b in TURN]
OTHER = [(0, 1), (1, 0)]


def nn(a, b):
    return jnp.dot(a, b, preferred_element_type=F32)


def nt(a, b):
    return lax.dot_general(a, b, (((1,), (1,)), ((), ())), preferred_element_type=F32)


def tn(a, b):
    return lax.dot_general(a, b, (((0,), (0,)), ((), ())), preferred_element_type=F32)


def dot(spec, a, b):
    return jnp.einsum(spec, a, b, preferred_element_type=F32)


def rows_of(every):
    n, both, d = every.shape
    half = both // 2
    return every[:, :half].reshape(n * half, d), every[:, half:].reshape(n * half, d)


def reorder(slots):
    n_z = slots // 2
    row = lax.broadcasted_iota(jnp.int32, (slots, slots), 0)
    column = lax.broadcasted_iota(jnp.int32, (slots, slots), 1)
    last = (row >= n_z).astype(jnp.int32)
    return (column == 2 * (row - n_z * last) + last).astype(F32).astype(BF)


def expert_kernel(every, mine, other, terms, rows, hidden, g_pre, h_part, g_part, win, wout, made, sems):
    hid = mine.shape[0] // 2
    n, both, d = every.shape
    half = both // 2
    loads = [pltpu.make_async_copy(other.at[:hid], win, sems.at[0]), pltpu.make_async_copy(other.at[hid:], wout, sems.at[1])]
    for load in loads:
        load.start()
    saves = []
    x, g = rows_of(every[...])
    for i in range(2):
        if i == 0:
            a, b = mine[:hid], mine[hid:]
        else:
            for load in loads:
                load.wait()
            saves.append(pltpu.make_async_copy(every, rows, sems.at[2]))
            saves[-1].start()
            a, b = win[...], wout[...]
        pre = nt(x, a)
        cdf = 0.5 * (1.0 + lax.erf(pre * 0.7071067811865476))
        h_part[i] = (pre * cdf).astype(BF)
        slope = cdf + pre * jnp.exp(-0.5 * pre * pre) * 0.3989422804014327
        g_part[i] = (nt(g, b) * slope).astype(BF)
        saves.append(pltpu.make_async_copy(h_part.at[i], hidden.at[i], sems.at[3 + 2 * i]))
        saves.append(pltpu.make_async_copy(g_part.at[i], g_pre.at[i], sems.at[4 + 2 * i]))
        saves[-2].start()
        saves[-1].start()
    out = nn(h_part[0], mine[hid:]) + nn(h_part[1], wout[...])
    made[:, :half] = out.astype(BF).reshape(n, half, d)
    saves.append(pltpu.make_async_copy(made.at[:, :half], terms.at[:, :half], sems.at[7]))
    saves[-1].start()
    back = nn(g_part[0], mine[:hid]) + nn(g_part[1], win[...])
    made[:, half:] = back.astype(BF).reshape(n, half, d)
    saves.append(pltpu.make_async_copy(made.at[:, half:], terms.at[:, half:], sems.at[8]))
    saves[-1].start()
    for save in saves:
        save.wait()


def grads_kernel(every, hidden, g_pre, kept, given):
    hid = kept.shape[0] // 2
    x, g = rows_of(every[...])
    for i, grads in enumerate((kept, given)):
        grads[:hid] = tn(g_pre[i], x).astype(BF)
        grads[hid:] = tn(hidden[i], g).astype(BF)


def add_kernel(kept, given, grads_in, grads_out):
    hid = grads_in.shape[0]
    grads_in[...] = (kept[:hid].astype(F32) + given[:hid].astype(F32)).astype(BF)
    grads_out[...] = (kept[hid:].astype(F32) + given[hid:].astype(F32)).astype(BF)


def place_kernel(a, b, a_out, b_out):
    a_out[...] = a[...]
    b_out[...] = b[...]


def sum_kernel(terms, sums, made, sem):
    n, both, d = terms.shape
    n_z = both // 2
    for core in range(2):
        for kind in range(2):
            total = 0.0
            for chip in range(core, n, 2):
                total = total + terms[chip, kind * n_z : (kind + 1) * n_z].astype(F32)
            made[:, core * 2 + kind] = total.astype(BF)
    send = pltpu.make_async_copy(made, sums, sem)
    send.start()
    send.wait()


def tail_kernel(back, tok, cot, dispatch, combine, term, g_logits, g_slot):
    turn = reorder(2 * back.shape[0])
    slot_out = tn(turn, jnp.concatenate([back[:, 0], back[:, 2]], axis=0)).astype(BF)
    slot_grad = tn(turn, jnp.concatenate([back[:, 1], back[:, 3]], axis=0)).astype(BF)
    com, dis = combine[...], dispatch[...]
    g_comb = nt(slot_out, cot[...])
    g_clog = com * (g_comb - jnp.sum(com * g_comb, axis=0, keepdims=True))
    g_disp = nt(slot_grad, tok[...])
    g_dlog = dis * (g_disp - jnp.sum(dis * g_disp, axis=1, keepdims=True))
    g_log = (g_dlog + g_clog).astype(BF)
    g_logits[...] = g_log
    g_slot[...] = slot_grad
    made = nn(g_log, tok[...]).astype(BF)
    wide = term.shape[2]
    for i in range(2):
        term[:, i] = made[:, i * wide : (i + 1) * wide]


def tokens_kernel(dispatch, g_logits, g_slot, router, grads):
    made = tn(dispatch[...].astype(BF), g_slot[...]) + tn(g_logits[...], router[...])
    grads[...] = made.astype(BF)


def total_kernel(parts, out, made, sem):
    total = jnp.sum(parts[...].astype(F32), axis=0, keepdims=True)
    made[...] = jnp.broadcast_to(total, made.shape).astype(BF)
    send = pltpu.make_async_copy(made, out, sem)
    send.start()
    send.wait()


def router_kernel(parts, grads):
    wide = parts.shape[2]
    for i in range(2):
        grads[:, i * wide : (i + 1) * wide] = parts[:, i].astype(F32)


def call(kernel, outs, flops, *args, saved=(), scratch=(), far=(), vmem=8):
    moved = sum(a.size * a.dtype.itemsize for a in (*args, *outs, *saved))
    whole = pl.BlockSpec(memory_space=pltpu.VMEM)
    return pl.pallas_call(
        kernel,
        out_shape=[*outs, *(pltpu.HBM(a.shape, a.dtype) for a in saved)],
        in_specs=[pl.BlockSpec(memory_space=pltpu.HBM) if i in far else whole for i in range(len(args))],
        out_specs=[whole] * len(outs) + [pl.BlockSpec(memory_space=pltpu.HBM)] * len(saved),
        scratch_shapes=scratch,
        compiler_params=pltpu.CompilerParams(vmem_limit_bytes=vmem * 2**20),
        cost_estimate=pl.CostEstimate(flops=flops, bytes_accessed=moved, transcendentals=0),
    )(*args)


def like(shape, kind=BF):
    return jax.ShapeDtypeStruct(shape, kind)


def swap(x, axis):
    return lax.all_to_all(x, axis, split_axis=0, concat_axis=0, tiled=True)


def local(tokens, router, w_in, w_out, cotangent):
    n_z = lax.axis_size("z")
    n_plane = lax.axis_size(PLANE)
    n_chips = lax.axis_size(CHIPS)
    tok, cot = tokens[0], cotangent[0]
    n_tok, d = tok.shape
    slots = 2 * n_z
    hid = w_out.shape[1]
    dma = pltpu.SemaphoreType.DMA
    one = 2 * n_tok * slots * d

    logits = dot("td,ds->ts", tok, router)
    dispatch = jax.nn.softmax(logits, axis=0)
    combine = jax.nn.softmax(logits, axis=1)
    slot_in = dot("ts,td->sd", dispatch.astype(BF), tok).astype(BF)
    g_late = dot("ts,td->sd", combine.astype(BF), cot).astype(BF)

    rows = jnp.stack([slot_in.reshape(n_z, 2, d), g_late.reshape(n_z, 2, d)], axis=2).reshape(n_z, 4, d)
    mine = lax.ppermute(jnp.concatenate([w_in[0].T, w_out[0]], axis=0), PAIR, TURN)
    rows = swap(rows, "z")
    other = lax.ppermute(mine, "core", OTHER)
    rows = rows.reshape(n_z, 2, 2, d).transpose(1, 2, 0, 3).reshape(1, 2, 2 * n_z, d)
    both = like((n_plane, 2 * n_z, d))
    every = jnp.broadcast_to(rows, (n_plane // 2, 2, 2 * n_z, d)).reshape(both.shape)
    every = swap(every, PLANE)
    n_rows = n_plane * n_z
    unit = like((2, n_rows, hid))
    block = like((2 * hid, d))
    half = like((hid, d))
    work = 2 * n_rows * hid * d
    terms, rows, hidden, g_pre = call(
        expert_kernel,
        [],
        8 * work,
        every,
        mine,
        other,
        far=(2,),
        saved=[both, both, unit, unit],
        scratch=[pltpu.VMEM(a.shape, BF) for a in (unit, unit, half, half, both)] + [dma((9,))],
        vmem=16,
    )
    kept, given = call(grads_kernel, [block, block], 4 * work, rows, hidden, g_pre, vmem=12)
    given = lax.ppermute(given, "core", OTHER)

    terms = swap(terms, PLANE)
    (sums,) = call(
        sum_kernel,
        [],
        400 * one,
        terms,
        saved=[like((n_z, 4, d))],
        scratch=[pltpu.VMEM((n_z, 4, d), BF), dma],
    )
    home_in, home_out = call(add_kernel, [half, half], block.size, kept, given)
    home_in = lax.ppermute(home_in, PAIR, BACK)
    back = swap(sums, "z")
    term, g_logits, g_slot = call(
        tail_kernel,
        [like((slots, 2, d // 2)), like((slots, n_tok)), like((slots, d))],
        400 * one,
        back,
        tok,
        cot,
        dispatch.T,
        combine.T,
    )

    term = swap(term, CHIPS)
    row, home_in, home_out = lax.optimization_barrier((term, home_in, home_out))
    home_out = lax.ppermute(home_out, PAIR, BACK)
    few, many = like((n_z, 2, d // 2)), like((n_chips, 2, d // 2))
    (row,) = call(total_kernel, [], row.size, row, saved=[few], scratch=[pltpu.VMEM(few.shape, BF), dma])
    (row,) = call(
        total_kernel, [], 1200 * one, swap(row, "z"), saved=[many], scratch=[pltpu.VMEM(many.shape, BF), dma]
    )
    row, home_in, home_out = lax.optimization_barrier((row, home_in, home_out))
    grad_w_in, grad_w_out = call(place_kernel, [half, half], block.size, home_in, home_out)
    (grad_router,) = call(router_kernel, [like((slots, d), F32)], row.size, swap(row, CHIPS))
    (grad_tokens,) = call(tokens_kernel, [like((n_tok, d))], 2 * one, dispatch.T, g_logits, g_slot, router.T)
    return (grad_tokens[None], grad_router.T, grad_w_in.T[None], grad_w_out[None])


def solution(mesh):
    fine = Mesh(np.asarray(mesh.devices).reshape(4, 2, 2, 16, 2), ("x", "yh", "yl", "z", "core"))
    images = P(("x", "yh", "yl", "z", "core"), None, None)
    first = P(("z", "core"), None, ("x", "yh", "yl"))
    second = P(("z", "core"), ("x", "yh", "yl"), None)
    return jax.shard_map(
        local,
        mesh=fine,
        in_specs=(images, P(), first, second, images),
        out_specs=(images, P(), first, second),
        check_vma=False,
    )
```

```python
import jax
import jax.numpy as jnp
import numpy as np
from jax import lax
from jax.experimental import pallas as pl
from jax.experimental.pallas import tpu as pltpu
from jax.sharding import Mesh, PartitionSpec as P

BF = jnp.bfloat16
F32 = jnp.float32
PLANE = ("x", "yh", "yl")
CHIPS = ("core", "x", "yh", "yl")
PAIR = ("yl", "core")
TURN = [(2, 0), (0, 1), (1, 3), (3, 2)]
BACK = [(b, a) for a, b in TURN]
OTHER = [(0, 1), (1, 0)]


def nn(a, b):
    return jnp.dot(a, b, preferred_element_type=F32)


def nt(a, b):
    return lax.dot_general(a, b, (((1,), (1,)), ((), ())), preferred_element_type=F32)


def tn(a, b):
    return lax.dot_general(a, b, (((0,), (0,)), ((), ())), preferred_element_type=F32)


def dot(spec, a, b):
    return jnp.einsum(spec, a, b, preferred_element_type=F32)


def rows_of(every):
    n, both, d = every.shape
    half = both // 2
    return every[:, :half].reshape(n * half, d), every[:, half:].reshape(n * half, d)


def reorder(slots):
    n_z = slots // 2
    row = lax.broadcasted_iota(jnp.int32, (slots, slots), 0)
    column = lax.broadcasted_iota(jnp.int32, (slots, slots), 1)
    last = (row >= n_z).astype(jnp.int32)
    return (column == 2 * (row - n_z * last) + last).astype(F32).astype(BF)


def expert_kernel(every, mine, other, terms, rows, hidden, g_pre, h_part, g_part, win, wout, made, sems):
    hid = mine.shape[0] // 2
    n, both, d = every.shape
    half = both // 2
    loads = [pltpu.make_async_copy(other.at[:hid], win, sems.at[0]), pltpu.make_async_copy(other.at[hid:], wout, sems.at[1])]
    for load in loads:
        load.start()
    saves = []
    x, g = rows_of(every[...])
    for i in range(2):
        if i == 0:
            a, b = mine[:hid], mine[hid:]
        else:
            for load in loads:
                load.wait()
            saves.append(pltpu.make_async_copy(every, rows, sems.at[2]))
            saves[-1].start()
            a, b = win[...], wout[...]
        pre = nt(x, a)
        cdf = 0.5 * (1.0 + lax.erf(pre * 0.7071067811865476))
        h_part[i] = (pre * cdf).astype(BF)
        slope = cdf + pre * jnp.exp(-0.5 * pre * pre) * 0.3989422804014327
        g_part[i] = (nt(g, b) * slope).astype(BF)
        saves.append(pltpu.make_async_copy(h_part.at[i], hidden.at[i], sems.at[3 + 2 * i]))
        saves.append(pltpu.make_async_copy(g_part.at[i], g_pre.at[i], sems.at[4 + 2 * i]))
        saves[-2].start()
        saves[-1].start()
    out = nn(h_part[0], mine[hid:]) + nn(h_part[1], wout[...])
    made[:, :half] = out.astype(BF).reshape(n, half, d)
    saves.append(pltpu.make_async_copy(made.at[:, :half], terms.at[:, :half], sems.at[7]))
    saves[-1].start()
    back = nn(g_part[0], mine[:hid]) + nn(g_part[1], win[...])
    made[:, half:] = back.astype(BF).reshape(n, half, d)
    saves.append(pltpu.make_async_copy(made.at[:, half:], terms.at[:, half:], sems.at[8]))
    saves[-1].start()
    for save in saves:
        save.wait()


def grads_kernel(every, hidden, g_pre, kept, given):
    hid = kept.shape[0] // 2
    x, g = rows_of(every[...])
    for i, grads in enumerate((kept, given)):
        grads[:hid] = tn(g_pre[i], x).astype(BF)
        grads[hid:] = tn(hidden[i], g).astype(BF)


def add_kernel(kept, given, grads_in, grads_out):
    hid = grads_in.shape[0]
    grads_in[...] = (kept[:hid].astype(F32) + given[:hid].astype(F32)).astype(BF)
    grads_out[...] = (kept[hid:].astype(F32) + given[hid:].astype(F32)).astype(BF)


def place_kernel(a, b, a_out, b_out):
    a_out[...] = a[...]
    b_out[...] = b[...]


def sum_kernel(terms, sums, made, sem):
    n, both, d = terms.shape
    n_z = both // 2
    for core in range(2):
        for kind in range(2):
            total = 0.0
            for chip in range(core, n, 2):
                total = total + terms[chip, kind * n_z : (kind + 1) * n_z].astype(F32)
            made[:, core * 2 + kind] = total.astype(BF)
    send = pltpu.make_async_copy(made, sums, sem)
    send.start()
    send.wait()


def tail_kernel(back, tok, cot, dispatch, combine, term, g_logits, g_slot):
    turn = reorder(2 * back.shape[0])
    slot_out = tn(turn, jnp.concatenate([back[:, 0], back[:, 2]], axis=0)).astype(BF)
    slot_grad = tn(turn, jnp.concatenate([back[:, 1], back[:, 3]], axis=0)).astype(BF)
    com, dis = combine[...], dispatch[...]
    g_comb = nt(slot_out, cot[...])
    g_clog = com * (g_comb - jnp.sum(com * g_comb, axis=0, keepdims=True))
    g_disp = nt(slot_grad, tok[...])
    g_dlog = dis * (g_disp - jnp.sum(dis * g_disp, axis=1, keepdims=True))
    g_log = (g_dlog + g_clog).astype(BF)
    g_logits[...] = g_log
    g_slot[...] = slot_grad
    made = nn(g_log, tok[...]).astype(BF)
    wide = term.shape[2]
    for i in range(2):
        term[:, i] = made[:, i * wide : (i + 1) * wide]


def tokens_kernel(dispatch, g_logits, g_slot, router, grads):
    made = tn(dispatch[...].astype(BF), g_slot[...]) + tn(g_logits[...], router[...])
    grads[...] = made.astype(BF)


def total_kernel(parts, out, made, sem):
    total = jnp.sum(parts[...].astype(F32), axis=0, keepdims=True)
    made[...] = jnp.broadcast_to(total, made.shape).astype(BF)
    send = pltpu.make_async_copy(made, out, sem)
    send.start()
    send.wait()


def router_kernel(parts, grads):
    wide = parts.shape[2]
    for i in range(2):
        grads[:, i * wide : (i + 1) * wide] = parts[:, i].astype(F32)


def call(kernel, outs, flops, *args, saved=(), scratch=(), far=(), vmem=8):
    moved = sum(a.size * a.dtype.itemsize for a in (*args, *outs, *saved))
    whole = pl.BlockSpec(memory_space=pltpu.VMEM)
    return pl.pallas_call(
        kernel,
        out_shape=[*outs, *(pltpu.HBM(a.shape, a.dtype) for a in saved)],
        in_specs=[pl.BlockSpec(memory_space=pltpu.HBM) if i in far else whole for i in range(len(args))],
        out_specs=[whole] * len(outs) + [pl.BlockSpec(memory_space=pltpu.HBM)] * len(saved),
        scratch_shapes=scratch,
        compiler_params=pltpu.CompilerParams(vmem_limit_bytes=vmem * 2**20),
        cost_estimate=pl.CostEstimate(flops=flops, bytes_accessed=moved, transcendentals=0),
    )(*args)


def like(shape, kind=BF):
    return jax.ShapeDtypeStruct(shape, kind)


def swap(x, axis):
    return lax.all_to_all(x, axis, split_axis=0, concat_axis=0, tiled=True)


def local(tokens, router, w_in, w_out, cotangent):
    n_z = lax.axis_size("z")
    n_plane = lax.axis_size(PLANE)
    n_chips = lax.axis_size(CHIPS)
    tok, cot = tokens[0], cotangent[0]
    n_tok, d = tok.shape
    slots = 2 * n_z
    hid = w_out.shape[1]
    dma = pltpu.SemaphoreType.DMA
    one = 2 * n_tok * slots * d

    logits = dot("td,ds->ts", tok, router)
    dispatch = jax.nn.softmax(logits, axis=0)
    combine = jax.nn.softmax(logits, axis=1)
    slot_in = dot("ts,td->sd", dispatch.astype(BF), tok).astype(BF)
    g_late = dot("ts,td->sd", combine.astype(BF), cot).astype(BF)

    rows = jnp.stack([slot_in.reshape(n_z, 2, d), g_late.reshape(n_z, 2, d)], axis=2).reshape(n_z, 4, d)
    mine = lax.ppermute(jnp.concatenate([w_in[0].T, w_out[0]], axis=0), PAIR, TURN)
    rows = swap(rows, "z")
    other = lax.ppermute(mine, "core", OTHER)
    rows = rows.reshape(n_z, 2, 2, d).transpose(1, 2, 0, 3).reshape(1, 2, 2 * n_z, d)
    both = like((n_plane, 2 * n_z, d))
    every = jnp.broadcast_to(rows, (n_plane // 2, 2, 2 * n_z, d)).reshape(both.shape)
    every = swap(every, PLANE)
    n_rows = n_plane * n_z
    unit = like((2, n_rows, hid))
    block = like((2 * hid, d))
    half = like((hid, d))
    work = 2 * n_rows * hid * d
    terms, rows, hidden, g_pre = call(
        expert_kernel,
        [],
        8 * work,
        every,
        mine,
        other,
        far=(2,),
        saved=[both, both, unit, unit],
        scratch=[pltpu.VMEM(a.shape, BF) for a in (unit, unit, half, half, both)] + [dma((9,))],
        vmem=16,
    )
    kept, given = call(grads_kernel, [block, block], 4 * work, rows, hidden, g_pre, vmem=12)
    given = lax.ppermute(given, "core", OTHER)

    terms = swap(terms, PLANE)
    (sums,) = call(
        sum_kernel,
        [],
        400 * one,
        terms,
        saved=[like((n_z, 4, d))],
        scratch=[pltpu.VMEM((n_z, 4, d), BF), dma],
    )
    home_in, home_out = call(add_kernel, [half, half], block.size, kept, given)
    home_in = lax.ppermute(home_in, PAIR, BACK)
    back = swap(sums, "z")
    term, g_logits, g_slot = call(
        tail_kernel,
        [like((slots, 2, d // 2)), like((slots, n_tok)), like((slots, d))],
        400 * one,
        back,
        tok,
        cot,
        dispatch.T,
        combine.T,
    )

    term = swap(term, CHIPS)
    row, home_in, home_out = lax.optimization_barrier((term, home_in, home_out))
    home_out = lax.ppermute(home_out, PAIR, BACK)
    few, many = like((n_z, 2, d // 2)), like((n_chips, 2, d // 2))
    (row,) = call(total_kernel, [], row.size, row, saved=[few], scratch=[pltpu.VMEM(few.shape, BF), dma])
    (row,) = call(
        total_kernel, [], 1200 * one, swap(row, "z"), saved=[many], scratch=[pltpu.VMEM(many.shape, BF), dma]
    )
    row, home_in, home_out = lax.optimization_barrier((row, home_in, home_out))
    grad_w_in, grad_w_out = call(place_kernel, [half, half], block.size, home_in, home_out)
    (grad_router,) = call(router_kernel, [like((slots, d), F32)], row.size, swap(row, CHIPS))
    (grad_tokens,) = call(tokens_kernel, [like((n_tok, d))], 2 * one, dispatch.T, g_logits, g_slot, router.T)
    return (grad_tokens[None], grad_router.T, grad_w_in.T[None], grad_w_out[None])


def solution(mesh):
    fine = Mesh(np.asarray(mesh.devices).reshape(4, 2, 2, 16, 2), ("x", "yh", "yl", "z", "core"))
    images = P(("x", "yh", "yl", "z", "core"), None, None)
    first = P(("z", "core"), None, ("x", "yh", "yl"))
    second = P(("z", "core"), ("x", "yh", "yl"), None)
    return jax.shard_map(
        local,
        mesh=fine,
        in_specs=(images, P(), first, second, images),
        out_specs=(images, P(), first, second),
        check_vma=False,
    )
```

```python
import jax
import jax.numpy as jnp
import numpy as np
from jax import lax
from jax.experimental import pallas as pl
from jax.experimental.pallas import tpu as pltpu
from jax.sharding import Mesh, PartitionSpec as P

BF = jnp.bfloat16
F32 = jnp.float32
PLANE = ("x", "yh", "yl")
CHIPS = ("core", "x", "yh", "yl")
PAIR = ("yl", "core")
TURN = [(2, 0), (0, 1), (1, 3), (3, 2)]
BACK = [(b, a) for a, b in TURN]
OTHER = [(0, 1), (1, 0)]


def nn(a, b):
    return jnp.dot(a, b, preferred_element_type=F32)


def nt(a, b):
    return lax.dot_general(a, b, (((1,), (1,)), ((), ())), preferred_element_type=F32)


def tn(a, b):
    return lax.dot_general(a, b, (((0,), (0,)), ((), ())), preferred_element_type=F32)


def dot(spec, a, b):
    return jnp.einsum(spec, a, b, preferred_element_type=F32)


def rows_of(every):
    n, both, d = every.shape
    half = both // 2
    return every[:, :half].reshape(n * half, d), every[:, half:].reshape(n * half, d)


def reorder(slots):
    n_z = slots // 2
    row = lax.broadcasted_iota(jnp.int32, (slots, slots), 0)
    column = lax.broadcasted_iota(jnp.int32, (slots, slots), 1)
    last = (row >= n_z).astype(jnp.int32)
    return (column == 2 * (row - n_z * last) + last).astype(F32).astype(BF)


def expert_kernel(every, mine, other, terms, rows, hidden, g_pre, h_part, g_part, win, wout, made, sems):
    hid = mine.shape[0] // 2
    n, both, d = every.shape
    half = both // 2
    loads = [pltpu.make_async_copy(other.at[:hid], win, sems.at[0]), pltpu.make_async_copy(other.at[hid:], wout, sems.at[1])]
    for load in loads:
        load.start()
    saves = []
    x, g = rows_of(every[...])
    for i in range(2):
        if i == 0:
            a, b = mine[:hid], mine[hid:]
        else:
            loads[0].wait()
            a = win[...]
        pre = nt(x, a)
        cdf = 0.5 * (1.0 + lax.erf(pre * 0.7071067811865476))
        h_part[i] = (pre * cdf).astype(BF)
        slope = cdf + pre * jnp.exp(-0.5 * pre * pre) * 0.3989422804014327
        if i == 1:
            loads[1].wait()
            saves.append(pltpu.make_async_copy(every, rows, sems.at[2]))
            saves[-1].start()
            b = wout[...]
        g_part[i] = (nt(g, b) * slope).astype(BF)
        saves.append(pltpu.make_async_copy(h_part.at[i], hidden.at[i], sems.at[3 + 2 * i]))
        saves.append(pltpu.make_async_copy(g_part.at[i], g_pre.at[i], sems.at[4 + 2 * i]))
        saves[-2].start()
        saves[-1].start()
    out = nn(h_part[0], mine[hid:]) + nn(h_part[1], wout[...])
    made[:, :half] = out.astype(BF).reshape(n, half, d)
    saves.append(pltpu.make_async_copy(made.at[:, :half], terms.at[:, :half], sems.at[7]))
    saves[-1].start()
    back = nn(g_part[0], mine[:hid]) + nn(g_part[1], win[...])
    made[:, half:] = back.astype(BF).reshape(n, half, d)
    saves.append(pltpu.make_async_copy(made.at[:, half:], terms.at[:, half:], sems.at[8]))
    saves[-1].start()
    for save in saves:
        save.wait()


def grads_kernel(every, hidden, g_pre, kept, given):
    hid = kept.shape[0] // 2
    x, g = rows_of(every[...])
    for i, grads in enumerate((kept, given)):
        grads[:hid] = tn(g_pre[i], x).astype(BF)
        grads[hid:] = tn(hidden[i], g).astype(BF)


def add_kernel(kept, given, grads_in, grads_out):
    hid = grads_in.shape[0]
    grads_in[...] = (kept[:hid].astype(F32) + given[:hid].astype(F32)).astype(BF)
    grads_out[...] = (kept[hid:].astype(F32) + given[hid:].astype(F32)).astype(BF)


def place_kernel(a, b, a_out, b_out):
    a_out[...] = a[...]
    b_out[...] = b[...]


def sum_kernel(terms, sums, made, sem):
    n, both, d = terms.shape
    n_z = both // 2
    for core in range(2):
        for kind in range(2):
            total = 0.0
            for chip in range(core, n, 2):
                total = total + terms[chip, kind * n_z : (kind + 1) * n_z].astype(F32)
            made[:, core * 2 + kind] = total.astype(BF)
    send = pltpu.make_async_copy(made, sums, sem)
    send.start()
    send.wait()


def tail_kernel(back, tok, cot, dispatch, combine, term, g_logits, g_slot):
    turn = reorder(2 * back.shape[0])
    slot_out = tn(turn, jnp.concatenate([back[:, 0], back[:, 2]], axis=0)).astype(BF)
    slot_grad = tn(turn, jnp.concatenate([back[:, 1], back[:, 3]], axis=0)).astype(BF)
    com, dis = combine[...], dispatch[...]
    g_comb = nt(slot_out, cot[...])
    g_clog = com * (g_comb - jnp.sum(com * g_comb, axis=0, keepdims=True))
    g_disp = nt(slot_grad, tok[...])
    g_dlog = dis * (g_disp - jnp.sum(dis * g_disp, axis=1, keepdims=True))
    g_log = (g_dlog + g_clog).astype(BF)
    g_logits[...] = g_log
    g_slot[...] = slot_grad
    made = nn(g_log, tok[...]).astype(BF)
    wide = term.shape[2]
    for i in range(2):
        term[:, i] = made[:, i * wide : (i + 1) * wide]


def tokens_kernel(dispatch, g_logits, g_slot, router, grads):
    made = tn(dispatch[...].astype(BF), g_slot[...]) + tn(g_logits[...], router[...])
    grads[...] = made.astype(BF)


def total_kernel(parts, out, made, sem):
    total = jnp.sum(parts[...].astype(F32), axis=0, keepdims=True)
    made[...] = jnp.broadcast_to(total, made.shape).astype(BF)
    send = pltpu.make_async_copy(made, out, sem)
    send.start()
    send.wait()


def router_kernel(parts, grads):
    wide = parts.shape[2]
    for i in range(2):
        grads[:, i * wide : (i + 1) * wide] = parts[:, i].astype(F32)


def call(kernel, outs, flops, *args, saved=(), scratch=(), far=(), vmem=8):
    moved = sum(a.size * a.dtype.itemsize for a in (*args, *outs, *saved))
    whole = pl.BlockSpec(memory_space=pltpu.VMEM)
    return pl.pallas_call(
        kernel,
        out_shape=[*outs, *(pltpu.HBM(a.shape, a.dtype) for a in saved)],
        in_specs=[pl.BlockSpec(memory_space=pltpu.HBM) if i in far else whole for i in range(len(args))],
        out_specs=[whole] * len(outs) + [pl.BlockSpec(memory_space=pltpu.HBM)] * len(saved),
        scratch_shapes=scratch,
        compiler_params=pltpu.CompilerParams(vmem_limit_bytes=vmem * 2**20),
        cost_estimate=pl.CostEstimate(flops=flops, bytes_accessed=moved, transcendentals=0),
    )(*args)


def like(shape, kind=BF):
    return jax.ShapeDtypeStruct(shape, kind)


def swap(x, axis):
    return lax.all_to_all(x, axis, split_axis=0, concat_axis=0, tiled=True)


def local(tokens, router, w_in, w_out, cotangent):
    n_z = lax.axis_size("z")
    n_plane = lax.axis_size(PLANE)
    n_chips = lax.axis_size(CHIPS)
    tok, cot = tokens[0], cotangent[0]
    n_tok, d = tok.shape
    slots = 2 * n_z
    hid = w_out.shape[1]
    dma = pltpu.SemaphoreType.DMA
    one = 2 * n_tok * slots * d

    logits = dot("td,ds->ts", tok, router)
    dispatch = jax.nn.softmax(logits, axis=0)
    combine = jax.nn.softmax(logits, axis=1)
    slot_in = dot("ts,td->sd", dispatch.astype(BF), tok).astype(BF)
    g_late = dot("ts,td->sd", combine.astype(BF), cot).astype(BF)

    rows = jnp.stack([slot_in.reshape(n_z, 2, d), g_late.reshape(n_z, 2, d)], axis=2).reshape(n_z, 4, d)
    mine = lax.ppermute(jnp.concatenate([w_in[0].T, w_out[0]], axis=0), PAIR, TURN)
    rows = swap(rows, "z")
    other = lax.ppermute(mine, "core", OTHER)
    rows = rows.reshape(n_z, 2, 2, d).transpose(1, 2, 0, 3).reshape(1, 2, 2 * n_z, d)
    both = like((n_plane, 2 * n_z, d))
    every = jnp.broadcast_to(rows, (n_plane // 2, 2, 2 * n_z, d)).reshape(both.shape)
    every = swap(every, PLANE)
    n_rows = n_plane * n_z
    unit = like((2, n_rows, hid))
    block = like((2 * hid, d))
    half = like((hid, d))
    work = 2 * n_rows * hid * d
    terms, rows, hidden, g_pre = call(
        expert_kernel,
        [],
        8 * work,
        every,
        mine,
        other,
        far=(2,),
        saved=[both, both, unit, unit],
        scratch=[pltpu.VMEM(a.shape, BF) for a in (unit, unit, half, half, both)] + [dma((9,))],
        vmem=16,
    )
    kept, given = call(grads_kernel, [block, block], 4 * work, rows, hidden, g_pre, vmem=12)
    given = lax.ppermute(given, "core", OTHER)

    terms = swap(terms, PLANE)
    (sums,) = call(
        sum_kernel,
        [],
        400 * one,
        terms,
        saved=[like((n_z, 4, d))],
        scratch=[pltpu.VMEM((n_z, 4, d), BF), dma],
    )
    home_in, home_out = call(add_kernel, [half, half], block.size, kept, given)
    home_in = lax.ppermute(home_in, PAIR, BACK)
    back = swap(sums, "z")
    term, g_logits, g_slot = call(
        tail_kernel,
        [like((slots, 2, d // 2)), like((slots, n_tok)), like((slots, d))],
        400 * one,
        back,
        tok,
        cot,
        dispatch.T,
        combine.T,
    )

    term = swap(term, CHIPS)
    row, home_in, home_out = lax.optimization_barrier((term, home_in, home_out))
    home_out = lax.ppermute(home_out, PAIR, BACK)
    few, many = like((n_z, 2, d // 2)), like((n_chips, 2, d // 2))
    (row,) = call(total_kernel, [], row.size, row, saved=[few], scratch=[pltpu.VMEM(few.shape, BF), dma])
    (row,) = call(
        total_kernel, [], 1200 * one, swap(row, "z"), saved=[many], scratch=[pltpu.VMEM(many.shape, BF), dma]
    )
    row, home_in, home_out = lax.optimization_barrier((row, home_in, home_out))
    grad_w_in, grad_w_out = call(place_kernel, [half, half], block.size, home_in, home_out)
    (grad_router,) = call(router_kernel, [like((slots, d), F32)], row.size, swap(row, CHIPS))
    (grad_tokens,) = call(tokens_kernel, [like((n_tok, d))], 2 * one, dispatch.T, g_logits, g_slot, router.T)
    return (grad_tokens[None], grad_router.T, grad_w_in.T[None], grad_w_out[None])


def solution(mesh):
    fine = Mesh(np.asarray(mesh.devices).reshape(4, 2, 2, 16, 2), ("x", "yh", "yl", "z", "core"))
    images = P(("x", "yh", "yl", "z", "core"), None, None)
    first = P(("z", "core"), None, ("x", "yh", "yl"))
    second = P(("z", "core"), ("x", "yh", "yl"), None)
    return jax.shard_map(
        local,
        mesh=fine,
        in_specs=(images, P(), first, second, images),
        out_specs=(images, P(), first, second),
        check_vma=False,
    )
```
